128 devices in a mesh: row: 16 (over y_hi, z, core), col: 8 (over y_lo, x).
Axes of the slice: x: 4, y: 4 (y_hi: 2, y_lo: 2; y = y_hi * 2 + y_lo), z: 4, core: 2. Of those that a mesh axis runs over, the one named last changes fastest.
Arguments:
- density: bfloat16 [6144, 6144], P('row', 'col'), may hold values from -0.875 to 0.875
- pattern: int32 [48, 48], P('row', 'col'), may hold values 0 or 1
- keep_list: int32 [48, 48], P('row', 'col'), may hold values 0 or 1
Outputs:
- square: bfloat16 [6144, 6144], P('row', 'col')
- purified: bfloat16 [6144, 6144], P('row', 'col')
The draws below stay inside these ranges and needn't reach their ends.
All inputs are finite; a program needn't handle non-finite values. No bound on the sum of `pattern` or of `keep_list` on one device may be relied on, other than what follows from the above.
Results may differ from the reference program's by a relative error of at most 0.005.
Values may be sent and summed in bfloat16 or wider, within the bound.
A program may use at most 64 MiB of HBM per device.

```python
import jax
import jax.numpy as jnp

BS = 128
NB = 48
ORDER = 6144


def touch_ends(array, stream_key, smallest, top_value):
    spot = [jax.random.randint(jax.random.fold_in(stream_key, axis), (), 0, length) for axis, length in enumerate(array.shape)]
    longest = array.shape.index(max(array.shape))
    beside = spot[:longest] + [(spot[longest] + 1) % array.shape[longest]] + spot[longest + 1:]
    return array.at[tuple(spot)].set(smallest).at[tuple(beside)].set(top_value)


def block_scale(own_key, shape, shards, smallest, largest):
    def one(axis_at, shards_of):
        steps = jax.random.uniform(jax.random.fold_in(jax.random.fold_in(own_key, 6), axis_at), (shards_of,), jnp.float32, smallest / len(shards), largest / len(shards))
        return jnp.repeat(jnp.exp(steps), shape[axis_at] // shards_of).reshape((-1,) + (1,) * (len(shape) - axis_at - 1))

    level = one(*shards[0])
    for cut in shards[1:]:
        level = level * one(*cut)
    return level


def bell_draw(stream_key, dims, spread, reach, shards=(), held_as=jnp.bfloat16):
    array = spread * jax.random.normal(stream_key, dims, jnp.float32)
    if shards:
        array = array * block_scale(stream_key, dims, shards, -0.22, 0.18)
    return jnp.clip(array, -reach, reach).astype(held_as)


def setup_inputs(seed: int = 0) -> dict:
    key_list = jax.random.split(jax.random.key(seed), 4)
    density = bell_draw(key_list[0], (ORDER, ORDER), NB ** -0.5, 0.875, ((0, 16), (1, 8)))
    pattern = touch_ends((jax.random.randint(key_list[1], (NB, NB), 0, 2) < 1).astype(jnp.int32), jax.random.fold_in(key_list[1], 1), 0, 1)
    keep_list = touch_ends((jax.random.randint(key_list[2], (NB, NB), 0, 4) < 3).astype(jnp.int32), jax.random.fold_in(key_list[2], 1), 0, 1)
    return {"density": density, "pattern": pattern, "keep_list": keep_list}


def expand_mask(block_mask):
    return jnp.repeat(jnp.repeat(block_mask, BS, axis=0), BS, axis=1)


def reference(density, pattern, keep_list):
    masked = jnp.where(expand_mask(pattern) > 0, density, jnp.zeros_like(density))
    square = jnp.dot(masked, masked, preferred_element_type=jnp.float32).astype(jnp.bfloat16)
    square = jnp.where(expand_mask(keep_list) > 0, square, jnp.zeros_like(square))
    cubic = jnp.dot(square, masked, preferred_element_type=jnp.float32)
    purified = (3.0 * square.astype(jnp.float32) - 2.0 * cubic).astype(jnp.bfloat16)
    return square, purified
```

```python
import jax
import jax.numpy as jnp
from jax import lax
from jax.experimental import pallas as pl
from jax.experimental.pallas import tpu as pltpu
from jax.sharding import PartitionSpec as P

MESH = pl.DeviceIdType.MESH
BF16 = jnp.bfloat16
F32 = jnp.float32

Q = 4
CH = 4
SL = 3


def kernel(
    dens, pattern, keep, square_out, purified_out,
    left, right, acc, sq, part_out, part_in, acc2, part2_out, part2_in,
    x_send, x_recv, y_send, y_recv, z_send, z_recv, c_send, c_recv,
    p_send, p_recv, s_send, s_recv, r_send, r_recv,
):
    rows, cols = dens.shape
    bs = rows // pattern.shape[0]
    r = lax.axis_index("row")
    c = lax.axis_index("col")
    core = r % 2
    z = (r // 2) % Q
    yh = r // (2 * Q)
    x = c % Q
    yl = c // Q

    def device(yh_, z_, core_, yl_, x_):
        return ((yh_ * Q + z_) * 2 + core_, yl_ * Q + x_)

    x_up = device(yh, z, core, yl, (x + 1) % Q)
    x_down = device(yh, z, core, yl, (x + Q - 1) % Q)
    z_up = device(yh, (z + 1) % Q, core, yl, x)
    z_down = device(yh, (z + Q - 1) % Q, core, yl, x)
    sibling = device(yh, z, 1 - core, yl, x)
    pair = device(yh, z, core, 1 - yl, x)

    def plane(yh_, yl_):
        return device(yh_, z, core, yl_, x)

    barrier = pltpu.get_barrier_semaphore()
    friends = [
        x_up, x_down, z_up, z_down, sibling, pair,
        plane(1 - yh, yl), plane(1 - yh, 1 - yl),
    ]
    for friend in friends:
        pl.semaphore_signal(barrier, inc=1, device_id=friend, device_id_type=MESH)

    for i in range(rows // bs):
        for k in range(cols // bs):
            block = dens[i * bs:(i + 1) * bs, k * bs:(k + 1) * bs]
            left[x, pl.ds(i * bs, bs), pl.ds(k * bs, bs)] = jnp.where(
                pattern[i, k] > 0, block, jnp.zeros_like(block)
            )
    pl.semaphore_wait(barrier, len(friends))

    def remote(src, dst, send, recv, to):
        return pltpu.make_async_remote_copy(
            src_ref=src, dst_ref=dst, send_sem=send, recv_sem=recv, device_id=to, device_id_type=MESH
        )

    first = 1 - yl
    own = yl
    straight = yh == yl
    half = rows // 2
    ch = rows // CH
    hc = ch // 2

    def x_step1(up):
        return remote(left.at[x], left.at[x], x_send.at[up], x_recv.at[up], x_up if up == 0 else x_down)

    def x_step2(up):
        at = (x + Q - 1) % Q if up == 0 else (x + 1) % Q
        part = left.at[at, pl.ds(up * half, half)]
        return remote(part, part, x_send.at[2 + up], x_recv.at[2 + up], x_up if up == 0 else x_down)

    def y_copy(to, i, target, which):
        src = left.at[x, pl.ds(i * ch, ch)]
        dst = right.at[yl, z, core, pl.ds(i * ch, ch)]
        return remote(src, dst, y_send.at[target, i], y_recv.at[which, i], to)

    near = [plane(0, yh), plane(1, yh)]
    far = plane(1 - yh, yh)

    def y_wait(which, i):
        at = right.at[first if which == 0 else own, z, core, pl.ds(i * ch, ch)]
        remote(at, at, y_send.at[0, i], y_recv.at[which, i], pair).wait_recv()

    def z_step1(q, i, up):
        j = first if q == 0 else own
        at = right.at[j, z, core, pl.ds(i * ch, ch)]
        return remote(at, at, z_send.at[q, 0, up, i], z_recv.at[q, 0, up, i], z_up if up == 0 else z_down)

    def z_got1(q, i, up):
        j = first if q == 0 else own
        at = (z + Q - 1) % Q if up == 0 else (z + 1) % Q
        return right.at[j, at, core, pl.ds(i * ch, ch)]

    def z_wait1(q, i, up):
        at = z_got1(q, i, up)
        remote(at, at, z_send.at[q, 0, up, i], z_recv.at[q, 0, up, i], z_up).wait_recv()

    def z_step2(q, i, up):
        j = first if q == 0 else own
        at = (z + Q - 1) % Q if up == 0 else (z + 1) % Q
        part = right.at[j, at, core, pl.ds(i * ch + up * hc, hc)]
        return remote(part, part, z_send.at[q, 1, up, i], z_recv.at[q, 1, up, i], z_up if up == 0 else z_down)

    def z_wait2(q, i, up):
        j = first if q == 0 else own
        part = right.at[j, (z + 2) % Q, core, pl.ds(i * ch + up * hc, hc)]
        remote(part, part, z_send.at[q, 1, up, i], z_recv.at[q, 1, up, i], z_up).wait_recv()

    def c_copy(q, d):
        j = first if q == 0 else own
        at = right.at[j, (z + d) % Q, core]
        return remote(at, at, c_send.at[q, d], c_recv.at[q, d], sibling)

    def c_wait(q, d):
        j = first if q == 0 else own
        at = right.at[j, (z + d) % Q, 1 - core]
        remote(at, at, c_send.at[q, d], c_recv.at[q, d], sibling).wait_recv()

    x_step1(0).start()
    x_step1(1).start()

    @pl.when(jnp.logical_not(straight))
    def _():
        for i in range(CH):
            for target in range(2):
                y_copy(near[target], i, target, 0).start()

    @pl.when(straight)
    def _():
        for i in range(CH):
            y_copy(far, i, 0, 1).start()
        right[own, z, core] = left[x]

    for i in range(CH):
        y_wait(0, i)
        z_step1(0, i, 0).start()
        z_step1(0, i, 1).start()
        if i >= 1:
            for up in range(2):
                z_wait1(0, i - 1, up)
                z_step2(0, i - 1, up).start()
    c_copy(0, 0).start()
    for up in range(2):
        z_wait1(0, CH - 1, up)
        z_step2(0, CH - 1, up).start()
    c_copy(0, 3).start()
    c_copy(0, 1).start()

    @pl.when(jnp.logical_not(straight))
    def _():
        for i in range(CH):
            y_wait(1, i)

    for i in range(CH):
        z_step1(1, i, 0).start()
        z_step1(1, i, 1).start()
    c_copy(1, 0).start()

    for up in range(2):
        at = (x + Q - 1) % Q if up == 0 else (x + 1) % Q
        remote(left.at[at], left.at[at], x_send.at[up], x_recv.at[up], x_up).wait_recv()
        x_step2(up).start()

    for i in range(CH):
        for up in range(2):
            z_wait2(0, i, up)
    c_copy(0, 2).start()
    for up in range(2):
        part = left.at[(x + 2) % Q, pl.ds(up * half, half)]
        remote(part, part, x_send.at[2 + up], x_recv.at[2 + up], x_up).wait_recv()

    width = 256
    tiles = cols // width

    def product(q, d, start):
        j = first if q == 0 else own
        at = (z + d) % Q

        def body(n, carry):
            span = pl.ds(pl.multiple_of(n * width, width), width)
            value = jnp.dot(left[at], right[j, at, :, :, span].reshape(2 * rows, width), preferred_element_type=F32)
            if start:
                acc[:, span] = value
            else:
                acc[:, span] += value
            return carry

        lax.fori_loop(0, tiles, body, 0)

    for step, d in enumerate((0, 1, 3, 2)):
        c_wait(0, d)
        product(0, d, step == 0)
    part_out[...] = acc[...].astype(BF16)
    p_copy = remote(part_out, part_in, p_send, p_recv, pair)
    p_copy.start()

    for i in range(CH):
        for up in range(2):
            z_wait1(1, i, up)
            z_step2(1, i, up).start()
    c_copy(1, 3).start()
    c_copy(1, 1).start()
    for step, d in enumerate((0, 1, 3)):
        c_wait(1, d)
        product(1, d, step == 0)
    for i in range(CH):
        for up in range(2):
            z_wait2(1, i, up)
    c_copy(1, 2).start()
    c_wait(1, 2)
    product(1, 2, False)
    p_copy.wait_recv()

    for i in range(rows // bs):
        for k in range(cols // bs):
            at = (slice(i * bs, (i + 1) * bs), slice(k * bs, (k + 1) * bs))
            block = (acc[at] + part_in[at].astype(F32)).astype(BF16)
            block = jnp.where(keep[i, k] > 0, block, jnp.zeros_like(block))
            square_out[at] = block
            sq[x, pl.ds(i * bs, bs), pl.ds(k * bs, bs)] = block

    sl = rows // SL
    hs = sl // 2

    def s_step1(i, up):
        part = sq.at[x, pl.ds(i * sl, sl)]
        return remote(part, part, s_send.at[0, up, i], s_recv.at[0, up, i], x_up if up == 0 else x_down)

    def s_wait1(i, up):
        at = (x + Q - 1) % Q if up == 0 else (x + 1) % Q
        part = sq.at[at, pl.ds(i * sl, sl)]
        remote(part, part, s_send.at[0, up, i], s_recv.at[0, up, i], x_up).wait_recv()

    def s_step2(i, up):
        at = (x + Q - 1) % Q if up == 0 else (x + 1) % Q
        part = sq.at[at, pl.ds(i * sl + up * hs, hs)]
        return remote(part, part, s_send.at[1, up, i], s_recv.at[1, up, i], x_up if up == 0 else x_down)

    def s_wait2(i, up):
        part = sq.at[(x + 2) % Q, pl.ds(i * sl + up * hs, hs)]
        remote(part, part, s_send.at[1, up, i], s_recv.at[1, up, i], x_up).wait_recv()

    def r_copy(i):
        part = pl.ds(i * sl, sl)
        return remote(part2_out.at[part], part2_in.at[part], r_send.at[i], r_recv.at[i], pair)

    def cubic(i, j):
        part = pl.ds(i * sl, sl)

        def body(n, carry):
            span = pl.ds(pl.multiple_of(n * width, width), width)
            value = jnp.dot(sq[0, part], right[j, 0, :, :, span].reshape(2 * rows, width), preferred_element_type=F32)
            for k in range(1, Q):
                value += jnp.dot(sq[k, part], right[j, k, :, :, span].reshape(2 * rows, width), preferred_element_type=F32)
            if j is first:
                part2_out[part, span] = value.astype(BF16)
            else:
                acc2[part, span] = value
            return carry

        lax.fori_loop(0, tiles, body, 0)

    for up in range(2):
        s_step1(0, up).start()
    for i in range(SL):
        if i + 1 < SL:
            for up in range(2):
                s_step1(i + 1, up).start()
        for up in range(2):
            s_wait1(i, up)
            s_step2(i, up).start()
        if i >= 1:
            for up in range(2):
                s_wait2(i - 1, up)
            cubic(i - 1, first)
            r_copy(i - 1).start()
            cubic(i - 1, own)
    for up in range(2):
        s_wait2(SL - 1, up)
    cubic(SL - 1, first)
    r_copy(SL - 1).start()
    cubic(SL - 1, own)
    for i in range(SL):
        r_copy(i).wait_recv()
        part = slice(i * sl, (i + 1) * sl)
        total = acc2[part] + part2_in[part].astype(F32)
        purified_out[part] = (3.0 * square_out[part].astype(F32) - 2.0 * total).astype(BF16)

    for up in range(2):
        x_step1(up).wait_send()
        x_step2(up).wait_send()

    @pl.when(jnp.logical_not(straight))
    def _():
        for i in range(CH):
            for target in range(2):
                y_copy(near[target], i, target, 0).wait_send()

    @pl.when(straight)
    def _():
        for i in range(CH):
            y_copy(far, i, 0, 1).wait_send()

    for q in range(2):
        for i in range(CH):
            for up in range(2):
                z_step1(q, i, up).wait_send()
                z_step2(q, i, up).wait_send()
        for d in range(Q):
            c_copy(q, d).wait_send()
    p_copy.wait_send()
    for i in range(SL):
        for up in range(2):
            s_step1(i, up).wait_send()
            s_step2(i, up).wait_send()
        r_copy(i).wait_send()


def on_device(density, pattern, keep_list):
    rows, cols = density.shape
    dma = pltpu.SemaphoreType.DMA
    vmem = pl.BlockSpec(memory_space=pltpu.VMEM)
    smem = pl.BlockSpec(memory_space=pltpu.SMEM)
    block = jax.ShapeDtypeStruct((rows, cols), BF16)
    return pl.pallas_call(
        kernel,
        out_shape=(block, block),
        in_specs=[vmem, smem, smem],
        out_specs=(vmem, vmem),
        scratch_shapes=[
            pltpu.VMEM((Q, rows, cols), BF16),
            pltpu.VMEM((2, Q, 2, rows, cols), BF16),
            pltpu.VMEM((rows, cols), F32),
            pltpu.VMEM((Q, rows, cols), BF16),
            pltpu.VMEM((rows, cols), BF16),
            pltpu.VMEM((rows, cols), BF16),
            pltpu.VMEM((rows, cols), F32),
            pltpu.VMEM((rows, cols), BF16),
            pltpu.VMEM((rows, cols), BF16),
            dma((4,)), dma((4,)),
            dma((2, CH)), dma((2, CH)),
            dma((2, 2, 2, CH)), dma((2, 2, 2, CH)),
            dma((2, Q)), dma((2, Q)),
            dma, dma,
            dma((2, 2, SL)), dma((2, 2, SL)),
            dma((SL,)), dma((SL,)),
        ],
        compiler_params=pltpu.CompilerParams(
            collective_id=0, has_side_effects=True, vmem_limit_bytes=48 * 1024 * 1024
        ),
    )(density, pattern, keep_list)


def solution(mesh):
    specs = P("row", "col")
    return jax.shard_map(
        on_device, mesh=mesh, in_specs=(specs,) * 3, out_specs=(specs,) * 2, check_vma=False
    )
```

```python
import jax
import jax.numpy as jnp
from jax import lax
from jax.experimental import pallas as pl
from jax.experimental.pallas import tpu as pltpu
from jax.sharding import PartitionSpec as P

MESH = pl.DeviceIdType.MESH
BF16 = jnp.bfloat16
F32 = jnp.float32

Q = 4
W = 256
CUTS = (0, 32, 128, 256, 384)


def kernel(
    dens_hbm, pattern_hbm, keep_hbm, square_out, purified_out,
    dens, pattern, keep, in_sem, left, mine, relay, right, acc, part_out, part_in, sq, acc2, part2_out, part2_in,
    x_send, x_recv, y_send, y_recv, w_recv, e_send, e_recv, z_send, z_recv, c_send, c_recv,
    p_send, p_recv, s_send, s_recv, t_send, t_recv, r_send, r_recv,
):
    loads = [
        pltpu.make_async_copy(src, dst, in_sem.at[i])
        for i, (src, dst) in enumerate(((dens_hbm, dens), (pattern_hbm, pattern), (keep_hbm, keep)))
    ]
    for load in loads:
        load.start()
    rows, cols = dens.shape
    bs = rows // pattern.shape[0]
    slices = cols // W
    half = rows // 2
    last = slices - 1
    r = lax.axis_index("row")
    c = lax.axis_index("col")
    core = r % 2
    z = (r // 2) % Q
    yh = r // (2 * Q)
    x = c % Q
    yl = c // Q
    straight = yh == yl
    bent = jnp.logical_not(straight)

    def device(yh_, z_, core_, yl_, x_):
        return ((yh_ * Q + z_) * 2 + core_, yl_ * Q + x_)

    def plane(yh_, yl_):
        return device(yh_, z, core, yl_, x)

    x_to = [device(yh, z, core, yl, (x + 1) % Q), device(yh, z, core, yl, (x + Q - 1) % Q)]
    z_to = [device(yh, (z + 1) % Q, core, yl, x), device(yh, (z + Q - 1) % Q, core, yl, x)]
    x_from = [(x + Q - 1) % Q, (x + 1) % Q]
    z_from = [(z + Q - 1) % Q, (z + 1) % Q]
    sibling = device(yh, z, 1 - core, yl, x)
    pair = plane(yh, 1 - yl)
    across = plane(1 - yh, 1 - yl)
    near = [plane(0, yh), plane(1, yh)]

    barrier = pltpu.get_barrier_semaphore()
    friends = x_to + z_to + [sibling, pair, across, plane(1 - yh, yl), device(yh, z, core, yl, (x + 2) % Q)]
    for friend in friends:
        pl.semaphore_signal(barrier, inc=1, device_id=friend, device_id_type=MESH)
    for load in loads:
        load.wait()

    for i in range(rows // bs):
        for k in range(cols // bs):
            block = dens[i * bs:(i + 1) * bs, k * bs:(k + 1) * bs]
            block = jnp.where(pattern[i, k] > 0, block, jnp.zeros_like(block))
            left[x, pl.ds(i * bs, bs), pl.ds(k * bs, bs)] = block
            n, at = divmod(k * bs, W)
            mine[n, i * bs:(i + 1) * bs, at:at + bs] = block
    pl.semaphore_wait(barrier, len(friends))

    def remote(src, dst, send, recv, to):
        return pltpu.make_async_remote_copy(
            src_ref=src, dst_ref=dst, send_sem=send, recv_sem=recv, device_id=to, device_id_type=MESH
        )

    def landing(at, send, recv):
        return remote(at, at, send, recv, pair)

    sent = []

    def go(copy):
        copy.start()
        sent.append(copy)

    first = 1 - yl
    own = yl

    def x_step1(which, up):
        part = left.at[x, pl.ds((up if which == 0 else 1 - up) * half, half)]
        return remote(part, part, x_send.at[which, up], x_recv.at[which, up], x_to[up])

    def x_wait1(which, up):
        part = left.at[x_from[up], pl.ds((up if which == 0 else 1 - up) * half, half)]
        landing(part, x_send.at[which, up], x_recv.at[which, up]).wait_recv()

    def x_step2(up):
        part = left.at[x_from[up], pl.ds(up * half, half)]
        return remote(part, part, x_send.at[2, up], x_recv.at[2, up], x_to[up])

    def x_begin():
        for up in range(2):
            go(x_step1(0, up))

    def x_middle():
        for up in range(2):
            x_wait1(0, up)
            go(x_step2(up))
            go(x_step1(1, up))

    def x_end():
        for up in range(2):
            x_wait1(1, up)
            part = left.at[(x + 2) % Q, pl.ds(up * half, half)]
            landing(part, x_send.at[2, up], x_recv.at[2, up]).wait_recv()

    bend = (yh + yl) % 2
    spare = 2 * slices

    def slot(j, n):
        return j * slices + n

    def y_part(n):
        return pl.ds(half, half) if n == last else pl.ds(0, rows)

    def y_near(n, t):
        at = right.at[slot(yl, n), z, core, y_part(n)]
        return remote(mine.at[n, y_part(n)], at, y_send.at[t, n], y_recv.at[0, n], near[t])

    def y_across(n):
        return remote(mine.at[n], relay.at[n], y_send.at[0, n], w_recv.at[n], across)

    def y_onward(n):
        at = right.at[slot(first, n), z, core]
        return remote(relay.at[n], at, y_send.at[1, n], y_recv.at[1, n], pair)

    def y_start(n):
        @pl.when(bent)
        def _():
            for t in range(2):
                y_near(n, t).start()

        if n == 0:
            @pl.when(straight)
            def _():
                y_across(n).start()

    def y_pass(n):
        @pl.when(straight)
        def _():
            y_across(n).wait_recv()
            y_onward(n).start()
            if n + 1 < slices:
                y_across(n + 1).start()

    def y_wait(n):
        at = right.at[slot(first, n), z, core, y_part(n)]
        landing(at, y_send.at[0, n], y_recv.at[0, n]).wait_recv()

    def y_wait_own(n):
        @pl.when(bent)
        def _():
            at = right.at[slot(own, n), z, core]
            landing(at, y_send.at[0, n], y_recv.at[1, n]).wait_recv()

    def e_copy(d, t):
        at = (z + d) % Q
        src = right.at[spare, at, core, pl.ds(0, half)]
        dst = right.at[slot(yl, last), at, core, pl.ds(0, half)]
        return remote(src, dst, e_send.at[d, t], e_recv.at[d], near[t])

    def e_start(d):
        @pl.when(bent)
        def _():
            for t in range(2):
                e_copy(d, t).start()

    def e_wait(d):
        at = right.at[slot(first, last), (z + d) % Q, core, pl.ds(0, half)]
        landing(at, e_send.at[d, 0], e_recv.at[d]).wait_recv()
        go(c_copy(EARLY, d))

    z_steps = [
        (bend * spare + (1 - bend) * slot(own, 0), 0, rows),
        (slot(first, 0), 0, rows),
        (slot(own, 1 - bend), 0, rows),
        (slot(first, 1), 0, rows),
        (slot(own, 2 - bend), 0, rows),
        (slot(first, last), half, half),
        (slot(own, last), 0, rows),
        (slot(first, last), 0, half),
    ]
    LAST, EARLY = 6, 7

    def z_piece(k, at, core_, part=None):
        s, lo, size = z_steps[k]
        if part is not None:
            size //= 2
            lo += part * size
        return right.at[s, at, core_, pl.ds(lo, size)]

    def z_step1(k, up):
        at = z_piece(k, z, core)
        return remote(at, at, z_send.at[0, k, up], z_recv.at[0, k, up], z_to[up])

    def z_wait1(k, up):
        landing(z_piece(k, z_from[up], core), z_send.at[0, k, up], z_recv.at[0, k, up]).wait_recv()

    def z_step2(k, up):
        part = z_piece(k, z_from[up], core, up)
        return remote(part, part, z_send.at[1, k, up], z_recv.at[1, k, up], z_to[up])

    def z_wait2(k, up):
        part = z_piece(k, (z + 2) % Q, core, up)
        landing(part, z_send.at[1, k, up], z_recv.at[1, k, up]).wait_recv()

    def c_copy(k, d):
        at = z_piece(k, (z + d) % Q, core)
        return remote(at, at, c_send.at[k, d], c_recv.at[k, d], sibling)

    def c_wait(k):
        for d in range(Q):
            at = z_piece(k, (z + d) % Q, 1 - core)
            landing(at, c_send.at[k, d], c_recv.at[k, d]).wait_recv()

    def z_begin(k):
        for up in range(2):
            go(z_step1(k, up))
        go(c_copy(k, 0))

    def z_middle(k):
        for up in range(2):
            z_wait1(k, up)
            go(z_step2(k, up))
        go(c_copy(k, 3))
        go(c_copy(k, 1))

    def z_end(k):
        for up in range(2):
            z_wait2(k, up)
        go(c_copy(k, 2))

    def f_begin():
        @pl.when(bent)
        def _():
            for up in range(2):
                z_step1(LAST, up).start()
            c_copy(LAST, 0).start()

    def f_middle():
        @pl.when(bent)
        def _():
            for up in range(2):
                z_wait1(LAST, up)
                z_step2(LAST, up).start()
            c_copy(LAST, 3).start()
            c_copy(LAST, 1).start()

    def f_end():
        @pl.when(bent)
        def _():
            for up in range(2):
                z_wait2(LAST, up)
            c_copy(LAST, 2).start()
            c_wait(LAST)

    def product(q, n):
        at = slot(first if q == 0 else own, n)
        value = None
        for k in range(Q):
            term = jnp.dot(left[k], right[at, k].reshape(2 * rows, W), preferred_element_type=F32)
            value = term if value is None else value + term
        if q == 0:
            part_out[n] = value.astype(BF16)
            go(p_copy(n))
        else:
            acc[...] = value

    def p_copy(n):
        return remote(part_out.at[n], part_in.at[n], p_send.at[n], p_recv.at[n], pair)

    def square(n):
        p_copy(n).wait_recv()
        for i in range(rows // bs):
            for k in range(W // bs):
                rs, cs = slice(i * bs, (i + 1) * bs), slice(k * bs, (k + 1) * bs)
                block = (acc[rs, cs] + part_in[n, rs, cs].astype(F32)).astype(BF16)
                block = jnp.where(keep[i, n * (W // bs) + k] > 0, block, jnp.zeros_like(block))
                square_out[rs, n * W + k * bs:n * W + (k + 1) * bs] = block
                sq[n, x, rs, cs] = block

    def s_step1(n, up):
        return remote(sq.at[n, x], sq.at[n, x], s_send.at[0, n, up], s_recv.at[0, n, up], x_to[up])

    def s_begin(n):
        for up in range(2):
            go(s_step1(n, up))

    def s_middle(n):
        for up in range(2):
            landing(sq.at[n, x_from[up]], s_send.at[0, n, up], s_recv.at[0, n, up]).wait_recv()
            part = sq.at[n, x_from[up], pl.ds(up * half, half)]
            go(remote(part, part, s_send.at[1, n, up], s_recv.at[1, n, up], x_to[up]))

    def s_end(n):
        for up in range(2):
            part = sq.at[n, (x + 2) % Q, pl.ds(up * half, half)]
            landing(part, s_send.at[1, n, up], s_recv.at[1, n, up]).wait_recv()

    def cubic(n, j, m, rs, start):
        lhs = jnp.concatenate([sq[n, k, rs] for k in range(Q)], axis=1)
        rhs = jnp.concatenate(
            [right[slot(j, m), k].reshape(2 * rows, W)[n * W:(n + 1) * W] for k in range(Q)], axis=0
        )
        value = jnp.dot(lhs, rhs, preferred_element_type=F32)
        if not start:
            value += acc2[0 if j is first else 1, m, rs]
        return value

    def cubic_add(q, n, m):
        acc2[q, m] = cubic(n, first if q == 0 else own, m, slice(0, rows), n == 0)

    def t_piece(i, at):
        return sq.at[last, at, pl.ds(CUTS[i], CUTS[i + 1] - CUTS[i])]

    def t_begin(i):
        for d in range(1, Q):
            to = device(yh, z, core, yl, (x + d) % Q)
            go(remote(t_piece(i, x), t_piece(i, x), t_send.at[i, d], t_recv.at[i, d], to))

    def t_end(i):
        for d in range(1, Q):
            landing(t_piece(i, (x + Q - d) % Q), t_send.at[i, d], t_recv.at[i, d]).wait_recv()

    def r_copy(i):
        part = pl.ds(CUTS[i], CUTS[i + 1] - CUTS[i])
        return remote(part2_out.at[:, part], part2_in.at[:, part], r_send.at[i], r_recv.at[i], pair)

    def cubic_last(i):
        rs = slice(CUTS[i], CUTS[i + 1])
        for m in range(slices):
            part2_out[m, rs] = cubic(last, first, m, rs, False).astype(BF16)
        go(r_copy(i))

    def purify(i):
        r_copy(i).wait_recv()
        rs = slice(CUTS[i], CUTS[i + 1])
        for m in range(slices):
            cs = slice(m * W, (m + 1) * W)
            total = acc2[1, m, rs] + part2_in[m, rs].astype(F32)
            purified_out[rs, cs] = (3.0 * square_out[rs, cs].astype(F32) - 2.0 * total).astype(BF16)

    x_begin()
    y_start(0)

    @pl.when(straight)
    def _():
        for n in range(slices):
            right[slot(own, n), z, core] = mine[n]

    @pl.when(bent)
    def _():
        right[spare, z, core] = mine[last]

    z_begin(0)
    z_middle(0)
    y_wait(0)
    z_begin(1)
    y_start(1)
    e_start(0)
    y_pass(0)
    x_middle()
    z_middle(1)
    y_wait_own(0)
    z_begin(2)
    y_pass(1)
    z_end(0)
    y_wait(1)
    z_begin(3)
    y_start(2)
    e_wait(0)
    e_start(1)
    z_middle(2)
    y_wait_own(1)
    z_begin(4)
    y_pass(2)
    z_end(1)
    x_end()
    c_wait(1)
    product(0, 0)
    y_wait(2)
    e_wait(1)
    e_start(3)
    e_start(2)
    z_middle(3)
    z_begin(5)
    z_end(2)
    c_wait(0)
    c_wait(2)
    product(1, 0)
    square(0)
    s_begin(0)
    z_middle(4)
    y_wait_own(2)
    f_begin()
    z_end(3)
    c_wait(3)
    product(0, 1)
    z_middle(5)
    s_middle(0)
    z_end(4)
    c_wait(4)
    product(1, 1)
    square(1)
    s_begin(1)
    f_middle()
    e_wait(3)
    e_wait(2)
    z_end(5)
    c_wait(5)
    c_wait(EARLY)
    product(0, 2)
    s_end(0)
    for m in range(slices):
        cubic_add(0, 0, m)
    f_end()
    product(1, 2)
    s_middle(1)
    square(2)
    t_begin(0)
    t_begin(1)
    s_end(1)
    for m in range(slices):
        cubic_add(0, 1, m)
    for i in range(len(CUTS) - 1):
        t_end(i)
        cubic_last(i)
        if i + 2 < len(CUTS) - 1:
            t_begin(i + 2)
    for m in range(slices):
        for n in range(last):
            cubic_add(1, n, m)
        acc2[1, m] = cubic(last, own, m, slice(0, rows), False)
    for i in range(len(CUTS) - 1):
        purify(i)

    for copy in sent:
        copy.wait_send()

    @pl.when(bent)
    def _():
        for t in range(2):
            for n in range(slices):
                y_near(n, t).wait_send()
            for d in range(Q):
                e_copy(d, t).wait_send()
        for up in range(2):
            z_step1(LAST, up).wait_send()
            z_step2(LAST, up).wait_send()
        for d in range(Q):
            c_copy(LAST, d).wait_send()

    @pl.when(straight)
    def _():
        for n in range(slices):
            y_across(n).wait_send()
            y_onward(n).wait_send()


def on_device(density, pattern, keep_list):
    rows, cols = density.shape
    slices = cols // W
    dma = pltpu.SemaphoreType.DMA
    vmem = pl.BlockSpec(memory_space=pltpu.VMEM)
    anywhere = pl.BlockSpec(memory_space=pl.ANY)
    block = jax.ShapeDtypeStruct((rows, cols), BF16)
    sliced = pltpu.VMEM((slices, rows, W), BF16)
    return pl.pallas_call(
        kernel,
        out_shape=(block, block),
        in_specs=[anywhere, anywhere, anywhere],
        out_specs=(vmem, vmem),
        scratch_shapes=[
            pltpu.VMEM((rows, cols), BF16),
            pltpu.SMEM(pattern.shape, pattern.dtype),
            pltpu.SMEM(keep_list.shape, keep_list.dtype),
            dma((3,)),
            pltpu.VMEM((Q, rows, cols), BF16),
            sliced,
            sliced,
            pltpu.VMEM((2 * slices + 1, Q, 2, rows, W), BF16),
            pltpu.VMEM((rows, W), F32),
            sliced,
            sliced,
            pltpu.VMEM((slices, Q, rows, W), BF16),
            pltpu.VMEM((2, slices, rows, W), F32),
            sliced,
            sliced,
            dma((3, 2)), dma((3, 2)),
            dma((2, slices)), dma((2, slices)), dma((slices,)),
            dma((Q, 2)), dma((Q,)),
            dma((2, 7, 2)), dma((2, 7, 2)),
            dma((8, Q)), dma((8, Q)),
            dma((slices,)), dma((slices,)),
            dma((2, slices, 2)), dma((2, slices, 2)),
            dma((len(CUTS) - 1, Q)), dma((len(CUTS) - 1, Q)),
            dma((len(CUTS) - 1,)), dma((len(CUTS) - 1,)),
        ],
        compiler_params=pltpu.CompilerParams(
            collective_id=0, has_side_effects=True, vmem_limit_bytes=48 * 1024 * 1024
        ),
    )(density, pattern, keep_list)


def solution(mesh):
    specs = P("row", "col")
    return jax.shard_map(
        on_device, mesh=mesh, in_specs=(specs,) * 3, out_specs=(specs,) * 2, check_vma=False
    )
```

```python
import jax
import jax.numpy as jnp
from jax import lax
from jax.experimental import pallas as pl
from jax.experimental.pallas import tpu as pltpu
from jax.sharding import PartitionSpec as P

MESH = pl.DeviceIdType.MESH
BF16 = jnp.bfloat16
F32 = jnp.float32

Q = 4
W = 256
CUTS = (0, 32, 128, 256, 384)


def kernel(
    dens_hbm, pattern_hbm, keep_hbm, square_out, purified_out,
    dens, pattern, keep, in_sem, left, mine, relay, right, acc, part_out, part_in, sq, acc2, part2_out, part2_in,
    x_send, x_recv, y_send, y_recv, w_recv, e_send, e_recv, z_send, z_recv, c_send, c_recv,
    p_send, p_recv, s_send, s_recv, t_send, t_recv, r_send, r_recv,
):
    loads = [
        pltpu.make_async_copy(src, dst, in_sem.at[i])
        for i, (src, dst) in enumerate(((dens_hbm, dens), (pattern_hbm, pattern), (keep_hbm, keep)))
    ]
    for load in loads:
        load.start()
    rows, cols = dens.shape
    bs = rows // pattern.shape[0]
    slices = cols // W
    half = rows // 2
    last = slices - 1
    r = lax.axis_index("row")
    c = lax.axis_index("col")
    core = r % 2
    z = (r // 2) % Q
    yh = r // (2 * Q)
    x = c % Q
    yl = c // Q
    straight = yh == yl
    bent = jnp.logical_not(straight)

    def device(yh_, z_, core_, yl_, x_):
        return ((yh_ * Q + z_) * 2 + core_, yl_ * Q + x_)

    def plane(yh_, yl_):
        return device(yh_, z, core, yl_, x)

    x_to = [device(yh, z, core, yl, (x + 1) % Q), device(yh, z, core, yl, (x + Q - 1) % Q)]
    z_to = [device(yh, (z + 1) % Q, core, yl, x), device(yh, (z + Q - 1) % Q, core, yl, x)]
    x_from = [(x + Q - 1) % Q, (x + 1) % Q]
    z_from = [(z + Q - 1) % Q, (z + 1) % Q]
    sibling = device(yh, z, 1 - core, yl, x)
    pair = plane(yh, 1 - yl)
    across = plane(1 - yh, 1 - yl)
    near = [plane(0, yh), plane(1, yh)]

    barrier = pltpu.get_barrier_semaphore()
    friends = x_to + z_to + [sibling, pair, across, plane(1 - yh, yl), device(yh, z, core, yl, (x + 2) % Q)]
    for friend in friends:
        pl.semaphore_signal(barrier, inc=1, device_id=friend, device_id_type=MESH)
    for load in loads:
        load.wait()

    for i in range(rows // bs):
        for k in range(cols // bs):
            block = dens[i * bs:(i + 1) * bs, k * bs:(k + 1) * bs]
            block = jnp.where(pattern[i, k] > 0, block, jnp.zeros_like(block))
            left[x, pl.ds(i * bs, bs), pl.ds(k * bs, bs)] = block
            n, at = divmod(k * bs, W)
            mine[n, i * bs:(i + 1) * bs, at:at + bs] = block
    pl.semaphore_wait(barrier, len(friends))

    def remote(src, dst, send, recv, to):
        return pltpu.make_async_remote_copy(
            src_ref=src, dst_ref=dst, send_sem=send, recv_sem=recv, device_id=to, device_id_type=MESH
        )

    def landing(at, send, recv):
        return remote(at, at, send, recv, pair)

    sent = []

    def go(copy):
        copy.start()
        sent.append(copy)

    def settle(young):
        while len(sent) > young:
            sent.pop(0).wait_send()

    first = 1 - yl
    own = yl

    def x_step1(which, up):
        part = left.at[x, pl.ds((up if which == 0 else 1 - up) * half, half)]
        return remote(part, part, x_send.at[which, up], x_recv.at[which, up], x_to[up])

    def x_wait1(which, up):
        part = left.at[x_from[up], pl.ds((up if which == 0 else 1 - up) * half, half)]
        landing(part, x_send.at[which, up], x_recv.at[which, up]).wait_recv()

    def x_step2(up):
        part = left.at[x_from[up], pl.ds(up * half, half)]
        return remote(part, part, x_send.at[2, up], x_recv.at[2, up], x_to[up])

    def x_begin():
        for up in range(2):
            go(x_step1(0, up))

    def x_middle():
        for up in range(2):
            x_wait1(0, up)
            go(x_step2(up))
            go(x_step1(1, up))

    def x_end():
        for up in range(2):
            x_wait1(1, up)
            part = left.at[(x + 2) % Q, pl.ds(up * half, half)]
            landing(part, x_send.at[2, up], x_recv.at[2, up]).wait_recv()

    bend = (yh + yl) % 2
    spare = 2 * slices

    def slot(j, n):
        return j * slices + n

    def y_part(n):
        return pl.ds(half, half) if n == last else pl.ds(0, rows)

    def y_near(n, t):
        at = right.at[slot(yl, n), z, core, y_part(n)]
        return remote(mine.at[n, y_part(n)], at, y_send.at[t, n], y_recv.at[0, n], near[t])

    def y_across(n):
        return remote(mine.at[n], relay.at[n], y_send.at[0, n], w_recv.at[n], across)

    def y_onward(n):
        at = right.at[slot(first, n), z, core]
        return remote(relay.at[n], at, y_send.at[1, n], y_recv.at[1, n], pair)

    def y_start(n):
        @pl.when(bent)
        def _():
            for t in range(2):
                y_near(n, t).start()

        if n == 0:
            @pl.when(straight)
            def _():
                y_across(n).start()

    def y_pass(n):
        @pl.when(straight)
        def _():
            y_across(n).wait_recv()
            y_onward(n).start()
            if n + 1 < slices:
                y_across(n + 1).start()

    def y_wait(n):
        at = right.at[slot(first, n), z, core, y_part(n)]
        landing(at, y_send.at[0, n], y_recv.at[0, n]).wait_recv()

    def y_wait_own(n):
        @pl.when(bent)
        def _():
            at = right.at[slot(own, n), z, core]
            landing(at, y_send.at[0, n], y_recv.at[1, n]).wait_recv()

    def e_copy(d, t):
        at = (z + d) % Q
        src = right.at[spare, at, core, pl.ds(0, half)]
        dst = right.at[slot(yl, last), at, core, pl.ds(0, half)]
        return remote(src, dst, e_send.at[d, t], e_recv.at[d], near[t])

    def e_start(d):
        @pl.when(bent)
        def _():
            for t in range(2):
                e_copy(d, t).start()

    def e_wait(d):
        at = right.at[slot(first, last), (z + d) % Q, core, pl.ds(0, half)]
        landing(at, e_send.at[d, 0], e_recv.at[d]).wait_recv()
        go(c_copy(EARLY, d))

    z_steps = [
        (bend * spare + (1 - bend) * slot(own, 0), 0, half),
        (slot(first, 0), 0, rows),
        (slot(own, 1 - bend), 0, rows),
        (slot(first, 1), 0, rows),
        (slot(own, 2 - bend), 0, rows),
        (slot(first, last), half, half),
        (slot(own, last), 0, rows),
        (slot(first, last), 0, half),
        (slot(own, 0), half, half),
    ]
    LAST, EARLY, OTHER = 6, 7, 8

    def z_piece(k, at, core_, part=None):
        s, lo, size = z_steps[k]
        if part is not None:
            size //= 2
            lo += part * size
        return right.at[s, at, core_, pl.ds(lo, size)]

    def z_step1(k, up):
        at = z_piece(k, z, core)
        return remote(at, at, z_send.at[0, k, up], z_recv.at[0, k, up], z_to[up])

    def z_wait1(k, up):
        landing(z_piece(k, z_from[up], core), z_send.at[0, k, up], z_recv.at[0, k, up]).wait_recv()

    def z_step2(k, up):
        part = z_piece(k, z_from[up], core, up)
        return remote(part, part, z_send.at[1, k, up], z_recv.at[1, k, up], z_to[up])

    def z_wait2(k, up):
        part = z_piece(k, (z + 2) % Q, core, up)
        landing(part, z_send.at[1, k, up], z_recv.at[1, k, up]).wait_recv()

    def c_copy(k, d):
        at = z_piece(k, (z + d) % Q, core)
        return remote(at, at, c_send.at[k, d], c_recv.at[k, d], sibling)

    def c_wait(k):
        for d in range(Q):
            at = z_piece(k, (z + d) % Q, 1 - core)
            landing(at, c_send.at[k, d], c_recv.at[k, d]).wait_recv()

    def z_begin(k):
        for up in range(2):
            go(z_step1(k, up))
        go(c_copy(k, 0))

    def z_middle(k):
        for up in range(2):
            z_wait1(k, up)
            go(z_step2(k, up))
        go(c_copy(k, 3))
        go(c_copy(k, 1))

    def z_end(k):
        for up in range(2):
            z_wait2(k, up)
        go(c_copy(k, 2))

    def f_begin():
        @pl.when(bent)
        def _():
            for up in range(2):
                z_step1(LAST, up).start()
            c_copy(LAST, 0).start()

    def f_middle():
        @pl.when(bent)
        def _():
            for up in range(2):
                z_wait1(LAST, up)
                z_step2(LAST, up).start()
            c_copy(LAST, 3).start()
            c_copy(LAST, 1).start()

    def f_end():
        @pl.when(bent)
        def _():
            for up in range(2):
                z_wait2(LAST, up)
            c_copy(LAST, 2).start()

    def f_shared():
        @pl.when(bent)
        def _():
            c_wait(LAST)

    def g_begin():
        @pl.when(straight)
        def _():
            for up in range(2):
                z_step1(OTHER, up).start()
            c_copy(OTHER, 0).start()

    def g_middle():
        @pl.when(straight)
        def _():
            for up in range(2):
                z_wait1(OTHER, up)
                z_step2(OTHER, up).start()
            c_copy(OTHER, 3).start()
            c_copy(OTHER, 1).start()

    def g_end():
        @pl.when(straight)
        def _():
            for up in range(2):
                z_wait2(OTHER, up)
            c_copy(OTHER, 2).start()
            c_wait(OTHER)

    def product(q, n):
        at = slot(first if q == 0 else own, n)
        value = None
        for k in range(Q):
            term = jnp.dot(left[k], right[at, k].reshape(2 * rows, W), preferred_element_type=F32)
            value = term if value is None else value + term
        if q == 0:
            part_out[n] = value.astype(BF16)
            go(p_copy(n))
        else:
            acc[...] = value

    def p_copy(n):
        return remote(part_out.at[n], part_in.at[n], p_send.at[n], p_recv.at[n], pair)

    def square(n):
        p_copy(n).wait_recv()
        for i in range(rows // bs):
            for k in range(W // bs):
                rs, cs = slice(i * bs, (i + 1) * bs), slice(k * bs, (k + 1) * bs)
                block = (acc[rs, cs] + part_in[n, rs, cs].astype(F32)).astype(BF16)
                block = jnp.where(keep[i, n * (W // bs) + k] > 0, block, jnp.zeros_like(block))
                square_out[rs, n * W + k * bs:n * W + (k + 1) * bs] = block
                sq[n, x, rs, cs] = block

    def s_step1(n, up):
        return remote(sq.at[n, x], sq.at[n, x], s_send.at[0, n, up], s_recv.at[0, n, up], x_to[up])

    def s_begin(n):
        for up in range(2):
            go(s_step1(n, up))

    def s_middle(n):
        for up in range(2):
            landing(sq.at[n, x_from[up]], s_send.at[0, n, up], s_recv.at[0, n, up]).wait_recv()
            part = sq.at[n, x_from[up], pl.ds(up * half, half)]
            go(remote(part, part, s_send.at[1, n, up], s_recv.at[1, n, up], x_to[up]))

    def s_end(n):
        for up in range(2):
            part = sq.at[n, (x + 2) % Q, pl.ds(up * half, half)]
            landing(part, s_send.at[1, n, up], s_recv.at[1, n, up]).wait_recv()

    def cubic(n, j, m, rs, start):
        lhs = jnp.concatenate([sq[n, k, rs] for k in range(Q)], axis=1)
        rhs = jnp.concatenate(
            [right[slot(j, m), k].reshape(2 * rows, W)[n * W:(n + 1) * W] for k in range(Q)], axis=0
        )
        value = jnp.dot(lhs, rhs, preferred_element_type=F32)
        if not start:
            value += acc2[0 if j is first else 1, m, rs]
        return value

    def cubic_add(q, n, m):
        acc2[q, m] = cubic(n, first if q == 0 else own, m, slice(0, rows), n == 0)

    def t_piece(i, at):
        return sq.at[last, at, pl.ds(CUTS[i], CUTS[i + 1] - CUTS[i])]

    def t_begin(i):
        for d in range(1, Q):
            to = device(yh, z, core, yl, (x + d) % Q)
            go(remote(t_piece(i, x), t_piece(i, x), t_send.at[i, d], t_recv.at[i, d], to))

    def t_end(i):
        for d in range(1, Q):
            landing(t_piece(i, (x + Q - d) % Q), t_send.at[i, d], t_recv.at[i, d]).wait_recv()

    def r_copy(i):
        part = pl.ds(CUTS[i], CUTS[i + 1] - CUTS[i])
        return remote(part2_out.at[:, part], part2_in.at[:, part], r_send.at[i], r_recv.at[i], pair)

    def cubic_last(i):
        rs = slice(CUTS[i], CUTS[i + 1])
        for m in range(slices):
            part2_out[m, rs] = cubic(last, first, m, rs, False).astype(BF16)
        go(r_copy(i))

    def purify(i):
        r_copy(i).wait_recv()
        rs = slice(CUTS[i], CUTS[i + 1])
        for m in range(slices):
            cs = slice(m * W, (m + 1) * W)
            total = acc2[1, m, rs] + part2_in[m, rs].astype(F32)
            purified_out[rs, cs] = (3.0 * square_out[rs, cs].astype(F32) - 2.0 * total).astype(BF16)

    x_begin()
    y_start(0)

    @pl.when(straight)
    def _():
        for n in range(slices):
            right[slot(own, n), z, core] = mine[n]

    @pl.when(bent)
    def _():
        right[spare, z, core] = mine[last]

    z_begin(0)
    g_begin()
    z_middle(0)
    y_wait(0)
    z_begin(1)
    y_start(1)
    e_start(0)
    y_pass(0)
    g_middle()
    x_middle()
    z_middle(1)
    y_wait_own(0)
    z_begin(2)
    y_pass(1)
    z_end(0)
    y_wait(1)
    z_begin(3)
    y_start(2)
    e_wait(0)
    e_start(1)
    z_middle(2)
    y_wait_own(1)
    z_begin(4)
    y_pass(2)
    z_end(1)
    x_end()
    c_wait(1)
    product(0, 0)
    y_wait(2)
    e_wait(1)
    e_start(3)
    e_start(2)
    settle(16)
    z_middle(3)
    z_begin(5)
    z_end(2)
    c_wait(0)
    c_wait(2)
    g_end()
    product(1, 0)
    square(0)
    s_begin(0)
    settle(16)
    z_middle(4)
    y_wait_own(2)
    f_begin()
    z_end(3)
    c_wait(3)
    product(0, 1)
    settle(16)
    z_middle(5)
    s_middle(0)
    z_end(4)
    c_wait(4)
    product(1, 1)
    square(1)
    s_begin(1)
    f_middle()
    e_wait(3)
    e_wait(2)
    z_end(5)
    c_wait(5)
    c_wait(EARLY)
    product(0, 2)
    s_end(0)
    for m in range(slices):
        cubic_add(0, 0, m)
    f_end()
    settle(16)
    s_middle(1)
    f_shared()
    product(1, 2)
    square(2)
    t_begin(0)
    t_begin(1)
    s_end(1)
    t_begin(2)
    for m in range(slices):
        cubic_add(0, 1, m)
    t_end(0)
    t_begin(3)
    cubic_last(0)
    for i in range(1, len(CUTS) - 1):
        t_end(i)
        cubic_last(i)
    for m in range(slices):
        for n in range(last):
            cubic_add(1, n, m)
        acc2[1, m] = cubic(last, own, m, slice(0, rows), False)
    settle(len(CUTS) - 1)

    @pl.when(bent)
    def _():
        for t in range(2):
            for n in range(slices):
                y_near(n, t).wait_send()
            for d in range(Q):
                e_copy(d, t).wait_send()
        for up in range(2):
            z_step1(LAST, up).wait_send()
            z_step2(LAST, up).wait_send()
        for d in range(Q):
            c_copy(LAST, d).wait_send()

    @pl.when(straight)
    def _():
        for n in range(slices):
            y_across(n).wait_send()
            y_onward(n).wait_send()
        for up in range(2):
            z_step1(OTHER, up).wait_send()
            z_step2(OTHER, up).wait_send()
        for d in range(Q):
            c_copy(OTHER, d).wait_send()

    for i in range(len(CUTS) - 1):
        purify(i)
    settle(0)


def on_device(density, pattern, keep_list):
    rows, cols = density.shape
    slices = cols // W
    dma = pltpu.SemaphoreType.DMA
    vmem = pl.BlockSpec(memory_space=pltpu.VMEM)
    anywhere = pl.BlockSpec(memory_space=pl.ANY)
    block = jax.ShapeDtypeStruct((rows, cols), BF16)
    sliced = pltpu.VMEM((slices, rows, W), BF16)
    return pl.pallas_call(
        kernel,
        out_shape=(block, block),
        in_specs=[anywhere, anywhere, anywhere],
        out_specs=(vmem, vmem),
        scratch_shapes=[
            pltpu.VMEM((rows, cols), BF16),
            pltpu.SMEM(pattern.shape, pattern.dtype),
            pltpu.SMEM(keep_list.shape, keep_list.dtype),
            dma((3,)),
            pltpu.VMEM((Q, rows, cols), BF16),
            sliced,
            sliced,
            pltpu.VMEM((2 * slices + 1, Q, 2, rows, W), BF16),
            pltpu.VMEM((rows, W), F32),
            sliced,
            sliced,
            pltpu.VMEM((slices, Q, rows, W), BF16),
            pltpu.VMEM((2, slices, rows, W), F32),
            sliced,
            sliced,
            dma((3, 2)), dma((3, 2)),
            dma((2, slices)), dma((2, slices)), dma((slices,)),
            dma((Q, 2)), dma((Q,)),
            dma((2, 9, 2)), dma((2, 9, 2)),
            dma((9, Q)), dma((9, Q)),
            dma((slices,)), dma((slices,)),
            dma((2, slices, 2)), dma((2, slices, 2)),
            dma((len(CUTS) - 1, Q)), dma((len(CUTS) - 1, Q)),
            dma((len(CUTS) - 1,)), dma((len(CUTS) - 1,)),
        ],
        compiler_params=pltpu.CompilerParams(
            collective_id=0, has_side_effects=True, vmem_limit_bytes=48 * 1024 * 1024
        ),
    )(density, pattern, keep_list)


def solution(mesh):
    specs = P("row", "col")
    return jax.shard_map(
        on_device, mesh=mesh, in_specs=(specs,) * 3, out_specs=(specs,) * 2, check_vma=False
    )
```

```python
import jax
import jax.numpy as jnp
from jax import lax
from jax.experimental import pallas as pl
from jax.experimental.pallas import tpu as pltpu
from jax.sharding import PartitionSpec as P

MESH = pl.DeviceIdType.MESH
BF16 = jnp.bfloat16
F32 = jnp.float32

Q = 4
W = 256
CUTS = (0, 64, 160, 288, 384)


def kernel(
    dens_hbm, pattern_hbm, keep_hbm, square_out, purified_out,
    dens, pattern, keep, in_sem, left, mine, relay, right, acc, part_out, part_in, sq, acc2, part2_out, part2_in,
    x_send, x_recv, y_send, y_recv, w_recv, e_send, e_recv, z_send, z_recv, c_send, c_recv,
    p_send, p_recv, s_send, s_recv, t_send, t_recv, r_send, r_recv,
):
    loads = [
        pltpu.make_async_copy(src, dst, in_sem.at[i])
        for i, (src, dst) in enumerate(((dens_hbm, dens), (pattern_hbm, pattern), (keep_hbm, keep)))
    ]
    for load in loads:
        load.start()
    rows, cols = dens.shape
    bs = rows // pattern.shape[0]
    slices = cols // W
    half = rows // 2
    last = slices - 1
    r = lax.axis_index("row")
    c = lax.axis_index("col")
    core = r % 2
    z = (r // 2) % Q
    yh = r // (2 * Q)
    x = c % Q
    yl = c // Q
    straight = yh == yl
    bent = jnp.logical_not(straight)

    def device(yh_, z_, core_, yl_, x_):
        return ((yh_ * Q + z_) * 2 + core_, yl_ * Q + x_)

    def plane(yh_, yl_):
        return device(yh_, z, core, yl_, x)

    x_to = [device(yh, z, core, yl, (x + 1) % Q), device(yh, z, core, yl, (x + Q - 1) % Q)]
    z_to = [device(yh, (z + 1) % Q, core, yl, x), device(yh, (z + Q - 1) % Q, core, yl, x)]
    x_from = [(x + Q - 1) % Q, (x + 1) % Q]
    z_from = [(z + Q - 1) % Q, (z + 1) % Q]
    sibling = device(yh, z, 1 - core, yl, x)
    pair = plane(yh, 1 - yl)
    across = plane(1 - yh, 1 - yl)
    near = [plane(0, yh), plane(1, yh)]

    barrier = pltpu.get_barrier_semaphore()
    friends = x_to + z_to + [sibling, pair, across, plane(1 - yh, yl), device(yh, z, core, yl, (x + 2) % Q)]
    for friend in friends:
        pl.semaphore_signal(barrier, inc=1, device_id=friend, device_id_type=MESH)
    for load in loads:
        load.wait()

    for i in range(rows // bs):
        for k in range(cols // bs):
            block = dens[i * bs:(i + 1) * bs, k * bs:(k + 1) * bs]
            block = jnp.where(pattern[i, k] > 0, block, jnp.zeros_like(block))
            left[x, pl.ds(i * bs, bs), pl.ds(k * bs, bs)] = block
            n, at = divmod(k * bs, W)
            mine[n, i * bs:(i + 1) * bs, at:at + bs] = block
    pl.semaphore_wait(barrier, len(friends))

    def remote(src, dst, send, recv, to):
        return pltpu.make_async_remote_copy(
            src_ref=src, dst_ref=dst, send_sem=send, recv_sem=recv, device_id=to, device_id_type=MESH
        )

    def landing(at, send, recv):
        return remote(at, at, send, recv, pair)

    sent = []

    def go(copy):
        copy.start()
        sent.append(copy)

    def settle(young):
        while len(sent) > young:
            sent.pop(0).wait_send()

    first = 1 - yl
    own = yl

    def x_step1(which, up):
        part = left.at[x, pl.ds((up if which == 0 else 1 - up) * half, half)]
        return remote(part, part, x_send.at[which, up], x_recv.at[which, up], x_to[up])

    def x_wait1(which, up):
        part = left.at[x_from[up], pl.ds((up if which == 0 else 1 - up) * half, half)]
        landing(part, x_send.at[which, up], x_recv.at[which, up]).wait_recv()

    def x_step2(up):
        part = left.at[x_from[up], pl.ds(up * half, half)]
        return remote(part, part, x_send.at[2, up], x_recv.at[2, up], x_to[up])

    def x_begin():
        for up in range(2):
            go(x_step1(0, up))

    def x_middle():
        for up in range(2):
            x_wait1(0, up)
            go(x_step2(up))
            go(x_step1(1, up))

    def x_end():
        for up in range(2):
            x_wait1(1, up)
            part = left.at[(x + 2) % Q, pl.ds(up * half, half)]
            landing(part, x_send.at[2, up], x_recv.at[2, up]).wait_recv()

    bend = (yh + yl) % 2
    spare = 2 * slices

    def slot(j, n):
        return j * slices + n

    def y_part(n):
        return pl.ds(half, half) if n == last else pl.ds(0, rows)

    def y_near(n, t):
        at = right.at[slot(yl, n), z, core, y_part(n)]
        return remote(mine.at[n, y_part(n)], at, y_send.at[t, n], y_recv.at[0, n], near[t])

    def y_across(n):
        return remote(mine.at[n], relay.at[n], y_send.at[0, n], w_recv.at[n], across)

    def y_onward(n):
        at = right.at[slot(first, n), z, core]
        return remote(relay.at[n], at, y_send.at[1, n], y_recv.at[1, n], pair)

    def y_start(n):
        @pl.when(bent)
        def _():
            for t in range(2):
                y_near(n, t).start()

        if n == 0:
            @pl.when(straight)
            def _():
                y_across(n).start()

    def y_pass(n):
        @pl.when(straight)
        def _():
            y_across(n).wait_recv()
            y_onward(n).start()
            if n + 1 < slices:
                y_across(n + 1).start()

    def y_wait(n):
        at = right.at[slot(first, n), z, core, y_part(n)]
        landing(at, y_send.at[0, n], y_recv.at[0, n]).wait_recv()

    def y_wait_own(n):
        @pl.when(bent)
        def _():
            at = right.at[slot(own, n), z, core]
            landing(at, y_send.at[0, n], y_recv.at[1, n]).wait_recv()

    def e_copy(d, t):
        at = (z + d) % Q
        src = right.at[spare, at, core, pl.ds(0, half)]
        dst = right.at[slot(yl, last), at, core, pl.ds(0, half)]
        return remote(src, dst, e_send.at[d, t], e_recv.at[d], near[t])

    def e_start(d):
        @pl.when(bent)
        def _():
            for t in range(2):
                e_copy(d, t).start()

    def e_wait(d):
        at = right.at[slot(first, last), (z + d) % Q, core, pl.ds(0, half)]
        landing(at, e_send.at[d, 0], e_recv.at[d]).wait_recv()
        go(c_copy(EARLY, d))

    z_steps = [
        (bend * spare + (1 - bend) * slot(own, 0), 0, half),
        (slot(first, 0), 0, rows),
        (slot(own, 1 - bend), 0, rows),
        (slot(first, 1), 0, rows),
        (slot(own, 2 - bend), 0, rows),
        (slot(first, last), half, half),
        (slot(own, last), 0, rows),
        (slot(first, last), 0, half),
        (slot(own, 0), half, half),
    ]
    LAST, EARLY, OTHER = 6, 7, 8

    def z_piece(k, at, core_, part=None):
        s, lo, size = z_steps[k]
        if part is not None:
            size //= 2
            lo += part * size
        return right.at[s, at, core_, pl.ds(lo, size)]

    def z_step1(k, up):
        at = z_piece(k, z, core)
        return remote(at, at, z_send.at[0, k, up], z_recv.at[0, k, up], z_to[up])

    def z_wait1(k, up):
        landing(z_piece(k, z_from[up], core), z_send.at[0, k, up], z_recv.at[0, k, up]).wait_recv()

    def z_step2(k, up):
        part = z_piece(k, z_from[up], core, up)
        return remote(part, part, z_send.at[1, k, up], z_recv.at[1, k, up], z_to[up])

    def z_wait2(k, up):
        part = z_piece(k, (z + 2) % Q, core, up)
        landing(part, z_send.at[1, k, up], z_recv.at[1, k, up]).wait_recv()

    def c_copy(k, d):
        at = z_piece(k, (z + d) % Q, core)
        return remote(at, at, c_send.at[k, d], c_recv.at[k, d], sibling)

    def c_wait(k):
        for d in range(Q):
            at = z_piece(k, (z + d) % Q, 1 - core)
            landing(at, c_send.at[k, d], c_recv.at[k, d]).wait_recv()

    def z_begin(k):
        for up in range(2):
            go(z_step1(k, up))
        go(c_copy(k, 0))

    def z_middle(k):
        for up in range(2):
            z_wait1(k, up)
            go(z_step2(k, up))
        go(c_copy(k, 3))
        go(c_copy(k, 1))

    def z_end(k):
        for up in range(2):
            z_wait2(k, up)
        go(c_copy(k, 2))

    def f_begin():
        @pl.when(bent)
        def _():
            for up in range(2):
                z_step1(LAST, up).start()
            c_copy(LAST, 0).start()

    def f_middle():
        @pl.when(bent)
        def _():
            for up in range(2):
                z_wait1(LAST, up)
                z_step2(LAST, up).start()
            c_copy(LAST, 3).start()
            c_copy(LAST, 1).start()

    def f_end():
        @pl.when(bent)
        def _():
            for up in range(2):
                z_wait2(LAST, up)
            c_copy(LAST, 2).start()

    def f_shared():
        @pl.when(bent)
        def _():
            c_wait(LAST)

    def g_begin():
        @pl.when(straight)
        def _():
            for up in range(2):
                z_step1(OTHER, up).start()
            c_copy(OTHER, 0).start()

    def g_middle():
        @pl.when(straight)
        def _():
            for up in range(2):
                z_wait1(OTHER, up)
                z_step2(OTHER, up).start()
            c_copy(OTHER, 3).start()
            c_copy(OTHER, 1).start()

    def g_end():
        @pl.when(straight)
        def _():
            for up in range(2):
                z_wait2(OTHER, up)
            c_copy(OTHER, 2).start()
            c_wait(OTHER)

    def product(q, n):
        at = slot(first if q == 0 else own, n)
        value = None
        for k in range(Q):
            term = jnp.dot(left[k], right[at, k].reshape(2 * rows, W), preferred_element_type=F32)
            value = term if value is None else value + term
        if q == 0:
            part_out[n] = value.astype(BF16)
            go(p_copy(n))
        else:
            acc[...] = value

    def p_copy(n):
        return remote(part_out.at[n], part_in.at[n], p_send.at[n], p_recv.at[n], pair)

    def square(n):
        p_copy(n).wait_recv()
        for i in range(rows // bs):
            for k in range(W // bs):
                rs, cs = slice(i * bs, (i + 1) * bs), slice(k * bs, (k + 1) * bs)
                block = (acc[rs, cs] + part_in[n, rs, cs].astype(F32)).astype(BF16)
                block = jnp.where(keep[i, n * (W // bs) + k] > 0, block, jnp.zeros_like(block))
                square_out[rs, n * W + k * bs:n * W + (k + 1) * bs] = block
                sq[n, x, rs, cs] = block

    def s_step1(n, up):
        return remote(sq.at[n, x], sq.at[n, x], s_send.at[0, n, up], s_recv.at[0, n, up], x_to[up])

    def s_begin(n):
        for up in range(2):
            go(s_step1(n, up))

    def s_middle(n):
        for up in range(2):
            landing(sq.at[n, x_from[up]], s_send.at[0, n, up], s_recv.at[0, n, up]).wait_recv()
            part = sq.at[n, x_from[up], pl.ds(up * half, half)]
            go(remote(part, part, s_send.at[1, n, up], s_recv.at[1, n, up], x_to[up]))

    def s_end(n):
        for up in range(2):
            part = sq.at[n, (x + 2) % Q, pl.ds(up * half, half)]
            landing(part, s_send.at[1, n, up], s_recv.at[1, n, up]).wait_recv()

    def cubic(n, j, m, rs, start):
        lhs = jnp.concatenate([sq[n, k, rs] for k in range(Q)], axis=1)
        rhs = jnp.concatenate(
            [right[slot(j, m), k].reshape(2 * rows, W)[n * W:(n + 1) * W] for k in range(Q)], axis=0
        )
        value = jnp.dot(lhs, rhs, preferred_element_type=F32)
        if not start:
            value += acc2[0 if j is first else 1, m, rs]
        return value

    def cubic_add(q, n, m):
        acc2[q, m] = cubic(n, first if q == 0 else own, m, slice(0, rows), n == 0)

    def t_piece(i, at):
        return sq.at[last, at, pl.ds(CUTS[i], CUTS[i + 1] - CUTS[i])]

    def t_begin(i):
        for d in range(1, Q):
            to = device(yh, z, core, yl, (x + d) % Q)
            go(remote(t_piece(i, x), t_piece(i, x), t_send.at[i, d], t_recv.at[i, d], to))

    def t_end(i):
        for d in range(1, Q):
            landing(t_piece(i, (x + Q - d) % Q), t_send.at[i, d], t_recv.at[i, d]).wait_recv()

    def r_copy(i):
        part = pl.ds(CUTS[i], CUTS[i + 1] - CUTS[i])
        return remote(part2_out.at[:, part], part2_in.at[:, part], r_send.at[i], r_recv.at[i], pair)

    def cubic_last(i):
        rs = slice(CUTS[i], CUTS[i + 1])
        for m in range(slices):
            part2_out[m, rs] = cubic(last, first, m, rs, False).astype(BF16)
        go(r_copy(i))

    def purify(i):
        r_copy(i).wait_recv()
        rs = slice(CUTS[i], CUTS[i + 1])
        for m in range(slices):
            cs = slice(m * W, (m + 1) * W)
            total = acc2[1, m, rs] + part2_in[m, rs].astype(F32)
            purified_out[rs, cs] = (3.0 * square_out[rs, cs].astype(F32) - 2.0 * total).astype(BF16)

    x_begin()
    y_start(0)

    @pl.when(straight)
    def _():
        for n in range(slices):
            right[slot(own, n), z, core] = mine[n]

    @pl.when(bent)
    def _():
        right[spare, z, core] = mine[last]

    z_begin(0)
    g_begin()
    z_middle(0)
    y_wait(0)
    z_begin(1)
    y_start(1)
    e_start(0)
    y_pass(0)
    g_middle()
    x_middle()
    z_middle(1)
    y_wait_own(0)
    z_begin(2)
    y_pass(1)
    z_end(0)
    y_wait(1)
    z_begin(3)
    y_start(2)
    e_wait(0)
    e_start(1)
    z_middle(2)
    y_wait_own(1)
    z_begin(4)
    y_pass(2)
    z_end(1)
    x_end()
    c_wait(1)
    product(0, 0)
    y_wait(2)
    e_wait(1)
    e_start(3)
    e_start(2)
    settle(16)
    z_middle(3)
    z_begin(5)
    z_end(2)
    c_wait(0)
    c_wait(2)
    g_end()
    product(1, 0)
    square(0)
    s_begin(0)
    settle(16)
    z_middle(4)
    y_wait_own(2)
    f_begin()
    z_end(3)
    c_wait(3)
    product(0, 1)
    settle(16)
    z_middle(5)
    s_middle(0)
    z_end(4)
    c_wait(4)
    product(1, 1)
    square(1)
    s_begin(1)
    f_middle()
    e_wait(3)
    e_wait(2)
    z_end(5)
    c_wait(5)
    c_wait(EARLY)
    product(0, 2)
    s_end(0)
    for m in range(slices):
        cubic_add(0, 0, m)
    f_end()
    settle(16)
    s_middle(1)
    f_shared()
    product(1, 2)
    square(2)
    t_begin(0)
    t_begin(1)
    s_end(1)
    t_begin(2)
    rest = CUTS[2]
    for m in range(slices):
        acc2[0, m, :rest] = cubic(1, first, m, slice(0, rest), False)
    t_end(0)
    t_begin(3)
    cubic_last(0)
    t_end(1)
    cubic_last(1)
    for m in range(slices):
        acc2[0, m, rest:] = cubic(1, first, m, slice(rest, rows), False)
    t_end(2)
    cubic_last(2)
    t_end(3)
    cubic_last(3)
    for m in range(slices):
        for n in range(last):
            cubic_add(1, n, m)
        acc2[1, m] = cubic(last, own, m, slice(0, rows), False)
    settle(len(CUTS) - 1)

    @pl.when(bent)
    def _():
        for t in range(2):
            for n in range(slices):
                y_near(n, t).wait_send()
            for d in range(Q):
                e_copy(d, t).wait_send()
        for up in range(2):
            z_step1(LAST, up).wait_send()
            z_step2(LAST, up).wait_send()
        for d in range(Q):
            c_copy(LAST, d).wait_send()

    @pl.when(straight)
    def _():
        for n in range(slices):
            y_across(n).wait_send()
            y_onward(n).wait_send()
        for up in range(2):
            z_step1(OTHER, up).wait_send()
            z_step2(OTHER, up).wait_send()
        for d in range(Q):
            c_copy(OTHER, d).wait_send()

    for i in range(len(CUTS) - 1):
        purify(i)
    settle(0)


def on_device(density, pattern, keep_list):
    rows, cols = density.shape
    slices = cols // W
    dma = pltpu.SemaphoreType.DMA
    vmem = pl.BlockSpec(memory_space=pltpu.VMEM)
    anywhere = pl.BlockSpec(memory_space=pl.ANY)
    block = jax.ShapeDtypeStruct((rows, cols), BF16)
    sliced = pltpu.VMEM((slices, rows, W), BF16)
    return pl.pallas_call(
        kernel,
        out_shape=(block, block),
        in_specs=[anywhere, anywhere, anywhere],
        out_specs=(vmem, vmem),
        scratch_shapes=[
            pltpu.VMEM((rows, cols), BF16),
            pltpu.SMEM(pattern.shape, pattern.dtype),
            pltpu.SMEM(keep_list.shape, keep_list.dtype),
            dma((3,)),
            pltpu.VMEM((Q, rows, cols), BF16),
            sliced,
            sliced,
            pltpu.VMEM((2 * slices + 1, Q, 2, rows, W), BF16),
            pltpu.VMEM((rows, W), F32),
            sliced,
            sliced,
            pltpu.VMEM((slices, Q, rows, W), BF16),
            pltpu.VMEM((2, slices, rows, W), F32),
            sliced,
            sliced,
            dma((3, 2)), dma((3, 2)),
            dma((2, slices)), dma((2, slices)), dma((slices,)),
            dma((Q, 2)), dma((Q,)),
            dma((2, 9, 2)), dma((2, 9, 2)),
            dma((9, Q)), dma((9, Q)),
            dma((slices,)), dma((slices,)),
            dma((2, slices, 2)), dma((2, slices, 2)),
            dma((len(CUTS) - 1, Q)), dma((len(CUTS) - 1, Q)),
            dma((len(CUTS) - 1,)), dma((len(CUTS) - 1,)),
        ],
        compiler_params=pltpu.CompilerParams(
            collective_id=0, has_side_effects=True, vmem_limit_bytes=48 * 1024 * 1024
        ),
    )(density, pattern, keep_list)


def solution(mesh):
    specs = P("row", "col")
    return jax.shard_map(
        on_device, mesh=mesh, in_specs=(specs,) * 3, out_specs=(specs,) * 2, check_vma=False
    )
```
